128 devices in a mesh: surf: 4 (over x), norm: 32 (over z, y, core).
Axes of the slice: x: 4, y: 4, z: 4, core: 2. Of those that a mesh axis runs over, the one named last changes fastest.
Arguments:
- rhs: float32 [128, 48, 512], P('norm', None, 'surf'), may hold values from -6 to 6
- previous: float32 [128, 48, 512], P('norm', None, 'surf'), may hold values from -6 to 6
- minus_jac: bfloat16 [128, 48, 48, 512], P('norm', None, None, 'surf'), may hold values from -0.4375 to 0.4375
- plus_jac: bfloat16 [128, 48, 48, 512], P('norm', None, None, 'surf'), may hold values from -0.4375 to 0.4375
- dissipation: float32 [128, 48, 512], P('norm', None, 'surf'), may hold values from 0.01 to 0.08
- inverse_diag: bfloat16 [128, 48, 48, 512], P('norm', None, None, 'surf'), may hold values from -0.078125 to 0.078125
- lower_coupling: bfloat16 [128, 48, 48, 512], P('norm', None, None, 'surf'), may hold values from -0.1484375 to 1, as said below
- upper_coupling: bfloat16 [128, 48, 48, 512], P('norm', None, None, 'surf'), may hold values from -0.1484375 to 1, as said below
Outputs:
- update: float32 [128, 48, 512], P('norm', None, 'surf')
The draws below stay inside these ranges and needn't reach their ends.
Inputs may be any that keep to these rules, and one draw needn't show every extreme that they name: `lower_coupling`: diagonal entries in (0, 1], off-diagonal entries small. `upper_coupling`: diagonal entries in (0, 1], off-diagonal entries small.
All inputs are finite; a program needn't handle non-finite values.
Results may differ from the reference program's by a relative error of at most 0.0003.
Values may be sent and summed in bfloat16 or wider, within the bound.
No kernel may reach another device: no remote copies, remote signals or barrier semaphores. Data moves between devices by JAX's collectives and lax.ppermute only.
A program may use at most 512 MiB of HBM per device.

```python
import math
import jax
import jax.numpy as jnp
from jax import lax

NEQ = 48
SWEEPS = 2
NS = 512
NORMAL_CELLS = 128


def coupling(key, low, high):
    random_key_list = jax.random.split(key, 3)
    unit_matrix = jnp.eye(NEQ, dtype=jnp.float32)[None, :, :, None]
    damping_rates = jnp.exp(jax.random.uniform(random_key_list[0], (1, NEQ, 1, NS), minval=math.log(low), maxval=math.log(high)))
    source_pulses = jnp.where(jax.random.uniform(random_key_list[1], (NORMAL_CELLS, 1, 1, 1)) < 3.0 / NORMAL_CELLS, 0.6, 1.0)
    species_blending = jnp.clip(0.03 * jax.random.normal(random_key_list[2], (NORMAL_CELLS, NEQ, NEQ, NS)), -0.1484375, 0.1484375)
    cell_block_set = unit_matrix * jnp.exp(-damping_rates / NORMAL_CELLS) * source_pulses + species_blending * (1.0 - unit_matrix)
    return cell_block_set.astype(jnp.bfloat16)


def draw_lower_coupling(key, part):
    key = jax.random.fold_in(key, 11)
    return coupling(key, 0.5, 24.0)


def draw_upper_coupling(key, part):
    key = jax.random.fold_in(key, 23)
    return coupling(key, 0.5, 24.0)


def steps_of(own_key, extent, cuts, smallest, high):
    loudness, own = 1.0, jax.random.fold_in(own_key, 6)
    for dim, parts in cuts:
        steps = jnp.exp(jax.random.uniform(jax.random.fold_in(own, dim), (parts,), jnp.float32, smallest / len(cuts), high / len(cuts)))
        loudness = loudness * jnp.repeat(steps, extent[dim] // parts).reshape([-1 if axis == dim else 1 for axis in range(len(extent))])
    return loudness


def centred(key, shape, deviation, most, shards=(), kind=jnp.bfloat16):
    loudness = steps_of(key, shape, shards, -0.22, 0.18) if shards else 1.0
    result = jax.random.normal(key, shape, jnp.float32) * deviation * loudness
    return jnp.minimum(jnp.maximum(result, -most), most).astype(kind)


def setup_inputs(seed: int = 0) -> dict:
    key_of = jax.random.split(jax.random.key(seed), 9)
    return {
        "rhs": centred(key_of[0], (NORMAL_CELLS, NEQ, NS), 1.0, 6.0, ((0, 32), (2, 4)), jnp.float32),
        "previous": centred(key_of[1], (NORMAL_CELLS, NEQ, NS), 1.0, 6.0, ((0, 32), (2, 4)), jnp.float32),
        "minus_jac": centred(key_of[2], (NORMAL_CELLS, NEQ, NEQ, NS), (4 * NEQ) ** -0.5, 0.4375, ((0, 32), (3, 4))),
        "plus_jac": centred(key_of[3], (NORMAL_CELLS, NEQ, NEQ, NS), (4 * NEQ) ** -0.5, 0.4375, ((0, 32), (3, 4))),
        "dissipation": jnp.clip(jnp.exp(math.log(0.08) - 2.0794415 * jax.random.uniform(key_of[4], (NORMAL_CELLS, NEQ, NS), jnp.float32) ** steps_of(key_of[4], (NORMAL_CELLS, NEQ, NS), ((0, 32), (2, 4)), -0.2, 0.2)), 0.01, 0.08),
        "inverse_diag": centred(key_of[5], (NORMAL_CELLS, NEQ, NEQ, NS), (NEQ * NORMAL_CELLS) ** -0.5, 0.078125, ((0, 32), (3, 4))),
        "lower_coupling": draw_lower_coupling(jax.random.fold_in(key_of[8], 71), 0),
        "upper_coupling": draw_upper_coupling(jax.random.fold_in(key_of[8], 71), 0),
    }


HIGH = lax.Precision.HIGHEST


def matvec(block, vector):
    return jnp.einsum('abs,bs->as', block.astype(jnp.float32), vector, precision=HIGH)


def reference(rhs, previous, minus_jac, plus_jac, dissipation, inverse_diag, lower_coupling, upper_coupling):
    delta = previous
    width = rhs.shape[2]
    for sweep_index in range(SWEEPS):
        padded = jnp.pad(delta, ((0, 0), (0, 0), (2, 2)))
        left_two = padded[:, :, 0:width]
        left_one = padded[:, :, 1:width + 1]
        centre = padded[:, :, 2:width + 2]
        right_one = padded[:, :, 3:width + 3]
        right_two = padded[:, :, 4:width + 4]
        fourth = left_two - 4.0 * left_one + 6.0 * centre - 4.0 * right_one + right_two

        def per_cell(items):
            residual_cell, below, above, minus_block, plus_block, inverse_block = items
            return matvec(inverse_block, residual_cell - matvec(minus_block, below) - matvec(plus_block, above))

        source = lax.map(per_cell, (rhs - dissipation * fourth, left_one, right_one, minus_jac, plus_jac, inverse_diag))

        def advance(carry, items):
            source_cell, block = items
            value = source_cell + matvec(block, carry)
            return value, value

        start = jnp.zeros(rhs.shape[1:], jnp.float32)
        forward_last, forward_values = lax.scan(advance, start, (source, lower_coupling))
        backward_first, backward_values = lax.scan(advance, start, (forward_values, upper_coupling), reverse=True)
        delta = backward_values
    return delta
```

```python
import functools

import jax
import jax.numpy as jnp
from jax import lax
from jax.experimental import pallas as pl
from jax.experimental.pallas import tpu as pltpu
from jax.sharding import PartitionSpec as P

SWEEPS = 2
N = 48
CELLS = 4
LANES = 128
MAT = N * N
GROUPS = 32
COLS = LANES // GROUPS
ROWS = 72
VEC = 3 * ROWS
PACK = VEC + 8
F32 = jnp.float32
BF16 = jnp.bfloat16
LIMIT = 60 * 1024 * 1024


def params():
    return pltpu.CompilerParams(vmem_limit_bytes=LIMIT)


def whole():
    return pl.BlockSpec(memory_space=pltpu.VMEM)


def matmul_cells(left, right, out, add=None):
    def block(step, carry):
        base = pl.multiple_of(step * 4 * N, 8)
        sums = [None] * 4
        for b in range(N):
            vector = right[pl.ds(b * N, N), :]
            for k in range(4):
                term = left[pl.ds(base + k * N + b, 1), :] * vector
                sums[k] = term if sums[k] is None else sums[k] + term
        for k in range(4):
            where = pl.ds(pl.multiple_of(base + k * N, 8), N)
            value = sums[k]
            if add is not None:
                value = value + add[where, :]
            out[where, :] = value
        return carry

    lax.fori_loop(0, N // 4, block, 0)


def pack_matrix(mat, out, first):
    def column(c, lo, count):
        return mat[pl.ds(c + lo * N, count, stride=N), :]

    def main(r, carry):
        tile = jnp.concatenate(
            [column(r, 0, 48), column(32 + r, 0, 16), column(16 + r, 0, 48), column(32 + r, 16, 16)], axis=0
        ).T
        for i in range(COLS):
            out[pl.ds(first + i * 16 + r, GROUPS, stride=PACK), :] = tile[GROUPS * i : GROUPS * (i + 1)]
        return carry

    lax.fori_loop(0, 16, main, 0)

    def rest(r, carry):
        tile = jnp.concatenate(
            [column(32 + r, 32, 16), column(40 + r, 32, 16), jnp.zeros((96, LANES), F32)], axis=0
        ).T
        out[pl.ds(first + 64 + r, GROUPS, stride=PACK), :] = jnp.concatenate(
            [tile[GROUPS * i : GROUPS * (i + 1), 0:32] for i in range(COLS)], axis=1
        )
        return carry

    lax.fori_loop(0, 8, rest, 0)


def products_kernel(lower, upper, out, low, upp, work0, work1, work2, work3):
    for k in range(CELLS):
        def widen(r, carry):
            where = pl.ds(pl.multiple_of(r * N, 16), N)
            low[k, where, :] = lower[k, r].astype(F32)
            upp[k, where, :] = upper[k, r].astype(F32)
            return carry

        lax.fori_loop(0, N, widen, 0)
    matmul_cells(low.at[1], low.at[0], work0)
    matmul_cells(low.at[2], work0, work1)
    matmul_cells(low.at[3], work1, work2)
    pack_matrix(work2, out, 0)
    matmul_cells(upp.at[2], work2, work3, work1)
    matmul_cells(upp.at[1], work3, work1, work0)
    matmul_cells(upp.at[0], work1, work2, low.at[0])
    pack_matrix(work2, out, 2 * ROWS)
    matmul_cells(upp.at[2], upp.at[3], work0)
    matmul_cells(upp.at[1], work0, work1)
    matmul_cells(upp.at[0], work1, work2)
    pack_matrix(work2, out, ROWS)


def products(lower, upper):
    return pl.pallas_call(
        products_kernel,
        out_shape=jax.ShapeDtypeStruct((GROUPS * PACK, LANES), F32),
        in_specs=[whole(), whole()],
        out_specs=whole(),
        scratch_shapes=[pltpu.VMEM((CELLS, MAT, LANES), F32)] * 2 + [pltpu.VMEM((MAT, LANES), F32)] * 4,
        compiler_params=params(),
        name="products",
    )(lower, upper)


def matvec(block, vector):
    rows = []
    for a in range(N):
        part = block[a].astype(F32) * vector
        rows.append(jnp.sum(part, axis=0, keepdims=True))
    return jnp.concatenate(rows, axis=0)


def source_kernel(
    rhs, delta, below, above, minus, plus, dissipation, inverse, lower, upper, source, vectors, hold
):
    lane = lax.broadcasted_iota(jnp.int32, (N, LANES), 1)
    forward = jnp.zeros((N, LANES), F32)
    for k in range(CELLS):
        centre = delta[k]
        left = below[k]
        right = above[k]

        def shifted(by):
            here = pltpu.roll(centre, by % LANES, 1)
            if by > 0:
                return jnp.where(lane < by, pltpu.roll(left, by, 1), here)
            return jnp.where(lane >= LANES + by, pltpu.roll(right, by % LANES, 1), here)

        left_one, right_one = shifted(1), shifted(-1)
        fourth = shifted(2) - 4.0 * left_one + 6.0 * centre - 4.0 * right_one + shifted(-2)
        residual = rhs[k] - dissipation[k] * fourth
        residual = residual - matvec(minus.at[k], left_one) - matvec(plus.at[k], right_one)
        value = matvec(inverse.at[k], residual)
        source[k] = value
        forward = value + matvec(lower.at[k], forward) if k else value
        hold[k] = forward
    backward = hold[CELLS - 1]
    for k in range(CELLS - 2, -1, -1):
        backward = hold[k] + matvec(upper.at[k], backward)
    gap = jnp.zeros((16, LANES), F32)
    for row, value in ((0, forward), (COLS, backward)):
        tile = jnp.concatenate([value, gap, value, gap], axis=0).T
        for i in range(COLS):
            vectors[pl.ds(row + i, GROUPS, stride=8), :] = tile[GROUPS * i : GROUPS * (i + 1)]


def local_source(*arrays):
    return pl.pallas_call(
        source_kernel,
        out_shape=(
            jax.ShapeDtypeStruct((CELLS, N, LANES), F32),
            jax.ShapeDtypeStruct((GROUPS * 8, LANES), F32),
        ),
        in_specs=[whole()] * 10,
        out_specs=(whole(), whole()),
        scratch_shapes=[pltpu.VMEM((CELLS, N, LANES), F32)],
        compiler_params=params(),
        name="local_source",
    )(*arrays)


def finish_kernel(incoming, source, lower, upper, delta, hold):
    def incoming_line(row):
        rows = [incoming[pl.ds(row + i, GROUPS, stride=8), :] for i in range(COLS)]
        return jnp.concatenate(rows, axis=0).T[0:N]

    value = incoming_line(0)
    for k in range(CELLS):
        value = source[k] + matvec(lower.at[k], value)
        hold[k] = value
    value = incoming_line(COLS)
    for k in range(CELLS - 1, -1, -1):
        value = hold[k] + matvec(upper.at[k], value)
        delta[k] = value


def finish(*arrays):
    return pl.pallas_call(
        finish_kernel,
        out_shape=jax.ShapeDtypeStruct((CELLS, N, LANES), F32),
        in_specs=[whole()] * 4,
        out_specs=whole(),
        scratch_shapes=[pltpu.VMEM((CELLS, N, LANES), F32)],
        compiler_params=params(),
        name="finish",
    )(*arrays)


def split(value):
    high = value.astype(BF16)
    return high, (value - high.astype(F32)).astype(BF16)


def unpack_matrix(packed, d, first, weights):
    lane = lax.broadcasted_iota(jnp.int32, (16, LANES), 1)
    extra = packed[d, pl.ds(first + 64, 8), :]
    zeros = jnp.zeros((16, LANES), F32)
    for i in range(COLS):
        block = packed[d, pl.ds(first + 16 * i, 16), :]
        turned = pltpu.roll(block, 64, 1)
        low = jnp.where(lane < 64, block, turned)
        high = jnp.where(lane < 64, turned, block)
        tail = jnp.concatenate(
            [pltpu.roll(extra, (32 - 32 * i) % LANES, 1), pltpu.roll(extra, (16 - 32 * i) % LANES, 1)], axis=0
        )
        third = jnp.where(lane < 16, pltpu.roll(block, 80, 1), jnp.where(lane < 32, pltpu.roll(block, 32, 1), tail))
        third = jnp.where(lane < 64, third, pltpu.roll(third, 64, 1))
        both = jnp.concatenate([low, high, third, zeros], axis=0)
        first_part, second_part = split(both)
        weights[pl.ds(64 * i, 64), 0:LANES] = first_part
        weights[pl.ds(64 * i, 64), LANES : 2 * LANES] = second_part


def spread(value):
    row = lax.broadcasted_iota(jnp.int32, (8, 2 * LANES), 0)
    place = lax.broadcasted_iota(jnp.int32, (8, 2 * LANES), 1) // 64
    keep = jnp.logical_and(row == place, lax.rem(lax.broadcasted_iota(jnp.int32, (8, 2 * LANES), 1), 64) < N)
    wide = jnp.where(keep, jnp.concatenate([value, value], axis=1), 0.0)
    high = wide.astype(BF16).astype(F32)
    return jnp.concatenate([high, wide - high], axis=0).astype(BF16)


def apply(left, weights):
    out = jnp.dot(left, weights[...], preferred_element_type=F32)
    return (out[0:8, 0:LANES] + out[8:16, 0:LANES]) + (out[0:8, LANES:] + out[8:16, LANES:])


def solve_kernel(packed, vectors, out, weights_a, weights_g, weights_b, ends):
    row = lax.broadcasted_iota(jnp.int32, (8, LANES), 0)
    state = jnp.zeros((8, LANES), F32)

    def forward(d, state):
        unpack_matrix(packed, d, 0, weights_a)
        unpack_matrix(packed, d, 2 * ROWS, weights_g)
        left = spread(state)
        ends[d] = pltpu.roll(vectors[d], COLS, 0) + apply(left, weights_g)
        out[d] = state
        return vectors[d] + apply(left, weights_a)

    lax.fori_loop(0, GROUPS, forward, state)

    def backward(e, state):
        d = GROUPS - 1 - e
        unpack_matrix(packed, d, ROWS, weights_b)
        out[d] = jnp.where(row < COLS, out[d], pltpu.roll(state, COLS, 0))
        return ends[d] + apply(spread(state), weights_b)

    lax.fori_loop(0, GROUPS, backward, jnp.zeros((8, LANES), F32))


def solve(packed, vectors):
    return pl.pallas_call(
        solve_kernel,
        out_shape=jax.ShapeDtypeStruct((GROUPS, 8, LANES), F32),
        in_specs=[whole(), whole()],
        out_specs=whole(),
        scratch_shapes=[pltpu.VMEM((2 * LANES, 2 * LANES), BF16)] * 3 + [pltpu.VMEM((GROUPS, 8, LANES), F32)],
        compiler_params=params(),
        name="solve",
    )(packed, vectors)


def exchange(value):
    return lax.all_to_all(value, "norm", 0, 0, tiled=True)


def shards(
    rhs, previous, minus_jac, plus_jac, dissipation, inverse_diag, lower_coupling, upper_coupling
):
    ends = lax.axis_size("surf") - 1
    up = [(i, i + 1) for i in range(ends)]
    down = [(i + 1, i) for i in range(ends)]
    packed = exchange(products(lower_coupling, upper_coupling).reshape(GROUPS, PACK, LANES))
    delta = previous
    for sweep_index in range(SWEEPS):
        below = lax.ppermute(delta, "surf", up)
        above = lax.ppermute(delta, "surf", down)
        source, vectors = local_source(
            rhs, delta, below, above, minus_jac, plus_jac, dissipation, inverse_diag, lower_coupling, upper_coupling
        )
        vectors = exchange(vectors.reshape(GROUPS, 8, LANES))
        incoming = exchange(solve(packed, vectors))
        delta = finish(incoming.reshape(GROUPS * 8, LANES), source, lower_coupling, upper_coupling)
    return delta


def solution(mesh):
    line = P("norm", None, "surf")
    block = P("norm", None, None, "surf")
    return jax.shard_map(
        shards,
        mesh=mesh,
        in_specs=(line, line, block, block, line, block, block, block),
        out_specs=line,
        check_vma=False,
    )
```

```python
import functools

import jax
import jax.numpy as jnp
from jax import lax
from jax.experimental import pallas as pl
from jax.experimental.pallas import tpu as pltpu
from jax.sharding import PartitionSpec as P

SWEEPS = 2
N = 48
CELLS = 4
LANES = 128
MAT = N * N
GROUPS = 32
COLS = LANES // GROUPS
ROWS = 72
FIRST = ROWS + 8
F32 = jnp.float32
BF16 = jnp.bfloat16


def params(mebibytes, microseconds):
    cost = pl.CostEstimate(flops=int(microseconds * 1e9), bytes_accessed=0, transcendentals=0)
    return dict(
        compiler_params=pltpu.CompilerParams(vmem_limit_bytes=mebibytes * 1024 * 1024), cost_estimate=cost
    )


def whole():
    return pl.BlockSpec(memory_space=pltpu.VMEM)


def matmul_cells(left, right, out, add=None):
    def block(step, carry):
        base = pl.multiple_of(step * 4 * N, 8)
        sums = [None] * 4
        for b in range(N):
            vector = right[pl.ds(b * N, N), :]
            for k in range(4):
                term = left[pl.ds(base + k * N + b, 1), :] * vector
                sums[k] = term if sums[k] is None else sums[k] + term
        for k in range(4):
            where = pl.ds(pl.multiple_of(base + k * N, 8), N)
            value = sums[k]
            if add is not None:
                value = value + add[where, :]
            out[where, :] = value
        return carry

    lax.fori_loop(0, N // 4, block, 0)


def pack_matrix(mat, out, first, pitch):
    def column(c, lo, count):
        return mat[pl.ds(c + lo * N, count, stride=N), :]

    def main(r, carry):
        tile = jnp.concatenate(
            [column(r, 0, 48), column(32 + r, 0, 16), column(16 + r, 0, 48), column(32 + r, 16, 16)], axis=0
        ).T
        for i in range(COLS):
            out[pl.ds(first + i * 16 + r, GROUPS, stride=pitch), :] = tile[GROUPS * i : GROUPS * (i + 1)]
        return carry

    lax.fori_loop(0, 16, main, 0, unroll=4)

    def rest(r, carry):
        tile = jnp.concatenate(
            [column(32 + r, 32, 16), column(40 + r, 32, 16), jnp.zeros((96, LANES), F32)], axis=0
        ).T
        out[pl.ds(first + 64 + r, GROUPS, stride=pitch), :] = jnp.concatenate(
            [tile[GROUPS * i : GROUPS * (i + 1), 0:32] for i in range(COLS)], axis=1
        )
        return carry

    lax.fori_loop(0, 8, rest, 0, unroll=4)


def widen(narrow, wide):
    for k in range(CELLS):
        def row(r, carry):
            wide[k, pl.ds(pl.multiple_of(r * N, 16), N), :] = narrow[k, r].astype(F32)
            return carry

        lax.fori_loop(0, N, row, 0, unroll=4)


def anywhere():
    return pl.BlockSpec(memory_space=pl.ANY)


def forward_kernel(lower, after, out, chain, low, work, sems):
    widen(lower, low)
    copies = []

    def keep(k, ref):
        copies.append(pltpu.make_async_copy(ref, chain.at[k], sems.at[k]))
        copies[-1].start()

    keep(0, low.at[0])
    for k in range(1, CELLS):
        before = low.at[0] if k == 1 else work.at[k - 2]
        matmul_cells(low.at[k], before, work.at[k - 1])
        keep(k, work.at[k - 1])
    pack_matrix(work.at[CELLS - 2], out, 0, FIRST)
    for copy in copies:
        copy.wait()


def forward_products(lower, after):
    return pl.pallas_call(
        forward_kernel,
        out_shape=(
            jax.ShapeDtypeStruct((GROUPS * FIRST, LANES), F32),
            jax.ShapeDtypeStruct((CELLS, MAT, LANES), F32),
        ),
        in_specs=[whole(), anywhere()],
        out_specs=(whole(), anywhere()),
        scratch_shapes=[
            pltpu.VMEM((CELLS, MAT, LANES), F32),
            pltpu.VMEM((CELLS - 1, MAT, LANES), F32),
            pltpu.SemaphoreType.DMA((CELLS,)),
        ],
        name="forward_products",
        **params(20, 12),
    )(lower, after)


def backward_kernel(upper, after, out, upp, work0, work1):
    widen(upper, upp)
    matmul_cells(upp.at[2], upp.at[3], work0)
    matmul_cells(upp.at[1], work0, work1)
    matmul_cells(upp.at[0], work1, work0)
    pack_matrix(work0, out, 0, ROWS)


def across_kernel(upper, after, chain, out, upp, have, work0, work1, sems):
    copies = [pltpu.make_async_copy(chain.at[k], have.at[k], sems.at[k]) for k in range(CELLS)]
    for copy in copies[::-1]:
        copy.start()
    widen(upper, upp)
    copies[3].wait()
    copies[2].wait()
    matmul_cells(upp.at[2], have.at[3], work0, have.at[2])
    copies[1].wait()
    matmul_cells(upp.at[1], work0, work1, have.at[1])
    copies[0].wait()
    matmul_cells(upp.at[0], work1, work0, have.at[0])
    pack_matrix(work0, out, 0, ROWS)


def backward_products(upper, after, chain=None):
    work = [pltpu.VMEM((MAT, LANES), F32)] * 2
    cells = pltpu.VMEM((CELLS, MAT, LANES), F32)
    across = chain is not None
    return pl.pallas_call(
        across_kernel if across else backward_kernel,
        out_shape=jax.ShapeDtypeStruct((GROUPS * ROWS, LANES), F32),
        in_specs=[whole(), anywhere()] + [anywhere()] * across,
        out_specs=whole(),
        scratch_shapes=[cells] + [cells] * across + work + [pltpu.SemaphoreType.DMA((CELLS,))] * across,
        name="across_products" if across else "backward_products",
        **params(22, 14),
    )(*((upper, after, chain) if across else (upper, after)))


def fold(parts):
    row = lax.broadcasted_iota(jnp.int32, (8, LANES), 0)
    for width in (4, 2, 1):
        lower_half = (row & width) == 0
        parts = [
            jnp.where(lower_half, one, two)
            + jnp.where(lower_half, pltpu.roll(one, 8 - width, 0), pltpu.roll(two, width, 0))
            for one, two in zip(parts[:width], parts[width:])
        ]
    return parts[0]


def matvec(block, vector):
    tiles = []
    for first in range(0, N, 8):
        parts = []
        for a in range(first, first + 8):
            product = block[a].astype(F32) * vector
            parts.append(sum(product[b : b + 8] for b in range(8, N, 8)) + product[0:8])
        tiles.append(fold(parts))
    return jnp.concatenate(tiles, axis=0)


def write_edges(delta, low, high):
    gap = jnp.zeros((LANES - 2 * N, LANES), F32)
    tiles = [jnp.concatenate([delta[2 * p], delta[2 * p + 1], gap], axis=0).T for p in range(2)]
    empty = jnp.zeros((4, LANES), F32)
    low[...] = jnp.concatenate([tiles[0][0:2], tiles[1][0:2], empty], axis=0)
    high[...] = jnp.concatenate([tiles[0][LANES - 2 :], tiles[1][LANES - 2 :], empty], axis=0)


def edges(delta):
    return pl.pallas_call(
        write_edges,
        out_shape=(jax.ShapeDtypeStruct((8, LANES), F32),) * 2,
        in_specs=[whole()],
        out_specs=(whole(),) * 2,
        name="edges",
        **params(4, 1),
    )(delta)


def source_kernel(
    rhs, delta, below, above, minus, plus, dissipation, inverse, lower, upper, *rest
):
    source, vectors, hold = rest[-3:] if len(rest) == 3 else (rest[1], rest[4], rest[3])
    lane = lax.broadcasted_iota(jnp.int32, (N, LANES), 1)
    place = lax.axis_index("surf")
    gap = jnp.zeros((LANES - 8, LANES), F32)
    before = jnp.concatenate([jnp.where(place == 0, 0.0, below[...]), gap], axis=0).T
    after = jnp.concatenate([jnp.where(place == lax.axis_size("surf") - 1, 0.0, above[...]), gap], axis=0).T
    forward = jnp.zeros((N, LANES), F32)
    for k in range(CELLS):
        centre = delta[k]
        first = k // 2 * 2
        left = before[k % 2 * N : k % 2 * N + N]
        right = after[k % 2 * N : k % 2 * N + N]

        def shifted(by):
            here = pltpu.roll(centre, by % LANES, 1)
            if by > 0:
                return jnp.where(lane < by, pltpu.roll(left, (by - 2 - first) % LANES, 1), here)
            return jnp.where(lane >= LANES + by, pltpu.roll(right, (by - first) % LANES, 1), here)

        left_one, right_one = shifted(1), shifted(-1)
        fourth = shifted(2) - 4.0 * left_one + 6.0 * centre - 4.0 * right_one + shifted(-2)
        residual = rhs[k] - dissipation[k] * fourth
        residual = residual - matvec(minus.at[k], left_one) - matvec(plus.at[k], right_one)
        value = matvec(inverse.at[k], residual)
        source[k] = value
        forward = value + matvec(lower.at[k], forward) if k else value
        hold[k] = forward
    backward = hold[CELLS - 1]
    for k in range(CELLS - 2, -1, -1):
        backward = hold[k] + matvec(upper.at[k], backward)
    gap = jnp.zeros((16, LANES), F32)
    for row, value in ((0, forward), (COLS, backward)):
        tile = jnp.concatenate([value, gap, value, gap], axis=0).T
        for i in range(COLS):
            for g in range(0, GROUPS, 8):
                start = GROUPS * i + g
                vectors[pl.ds(g, 8), row + i, :] = tile[start : start + 8]


    if len(rest) > 3:
        copy = pltpu.make_async_copy(vectors, rest[2].at[:, pl.ds(ROWS, 8), :], rest[5])
        copy.start()
        copy.wait()


def local_source(*arrays, packed=None):
    lines = jax.ShapeDtypeStruct((CELLS, N, LANES), F32)
    hold = pltpu.VMEM((CELLS, N, LANES), F32)
    if packed is None:
        return pl.pallas_call(
            source_kernel,
            out_shape=(lines, jax.ShapeDtypeStruct((GROUPS, 8, LANES), F32)),
            in_specs=[whole()] * 10,
            out_specs=(whole(), whole()),
            scratch_shapes=[hold],
            name="local_source",
            **params(16, 3),
        )(*arrays)
    return pl.pallas_call(
        source_kernel,
        out_shape=(lines, jax.ShapeDtypeStruct(packed.shape, F32)),
        in_specs=[whole()] * 10 + [pl.BlockSpec(memory_space=pl.ANY)],
        out_specs=(whole(), pl.BlockSpec(memory_space=pl.ANY)),
        scratch_shapes=[hold, pltpu.VMEM((GROUPS, 8, LANES), F32), pltpu.SemaphoreType.DMA],
        input_output_aliases={10: 1},
        name="local_source_packed",
        **params(17, 3),
    )(*arrays, packed)


def finish_kernel(incoming, source, lower, upper, delta, *rest):
    hold = rest[-1]

    def incoming_line(row):
        rows = [incoming[pl.ds(row + i, GROUPS, stride=8), :] for i in range(COLS)]
        return jnp.concatenate(rows, axis=0).T[0:N]

    value = incoming_line(0)
    for k in range(CELLS):
        value = source[k] + matvec(lower.at[k], value)
        hold[k] = value
    value = incoming_line(COLS)
    for k in range(CELLS - 1, -1, -1):
        value = hold[k] + matvec(upper.at[k], value)
        delta[k] = value
    if len(rest) > 1:
        write_edges(delta, rest[0], rest[1])


def finish(last, *arrays):
    edge = jax.ShapeDtypeStruct((8, LANES), F32)
    results = (jax.ShapeDtypeStruct((CELLS, N, LANES), F32),) + (() if last else (edge, edge))
    return pl.pallas_call(
        finish_kernel,
        out_shape=results,
        in_specs=[whole()] * 4,
        out_specs=(whole(),) * len(results),
        scratch_shapes=[pltpu.VMEM((CELLS, N, LANES), F32)],
        name="finish",
        **params(8, 1.5),
    )(*arrays)


def split(value):
    high = value.astype(BF16)
    return high, (value - high.astype(F32)).astype(BF16)


def unpack_matrix(packed, d, first, weights):
    lane = lax.broadcasted_iota(jnp.int32, (16, LANES), 1)
    extra = packed[d, pl.ds(first + 64, 8), :]
    zeros = jnp.zeros((16, LANES), F32)
    for i in range(COLS):
        block = packed[d, pl.ds(first + 16 * i, 16), :]
        turned = pltpu.roll(block, 64, 1)
        low = jnp.where(lane < 64, block, turned)
        high = jnp.where(lane < 64, turned, block)
        tail = jnp.concatenate(
            [pltpu.roll(extra, (32 - 32 * i) % LANES, 1), pltpu.roll(extra, (16 - 32 * i) % LANES, 1)], axis=0
        )
        third = jnp.where(lane < 16, pltpu.roll(block, 80, 1), jnp.where(lane < 32, pltpu.roll(block, 32, 1), tail))
        third = jnp.where(lane < 64, third, pltpu.roll(third, 64, 1))
        both = jnp.concatenate([low, high, third, zeros], axis=0)
        first_part, second_part = split(both)
        weights[pl.ds(64 * i, 64), 0:LANES] = first_part
        weights[pl.ds(64 * i, 64), LANES : 2 * LANES] = second_part


def spread(value, keep):
    wide = jnp.where(keep, jnp.concatenate([value, value], axis=1), 0.0)
    high = wide.astype(BF16).astype(F32)
    return jnp.concatenate([high, wide - high], axis=0).astype(BF16)


def kept():
    row = lax.broadcasted_iota(jnp.int32, (8, 2 * LANES), 0)
    lane = lax.broadcasted_iota(jnp.int32, (8, 2 * LANES), 1)
    return jnp.logical_and(row == lane // 64, lax.rem(lane, 64) < N)


def apply(left, weights):
    out = jnp.dot(left, weights[...], preferred_element_type=F32)
    return (out[0:8, 0:LANES] + out[8:16, 0:LANES]) + (out[0:8, LANES:] + out[8:16, LANES:])


def forward_solve_kernel(packed, vectors, out, even, odd):
    weights = (even, odd)
    keep = kept()
    base = ROWS if vectors.shape[1] > 8 else 0
    unpack_matrix(packed, 0, 0, even)

    def pair(e, state):
        for side in range(2):
            d = 2 * e + side
            unpack_matrix(packed, jnp.minimum(d + 1, GROUPS - 1), 0, weights[1 - side])
            out[d] = state
            state = vectors[d, pl.ds(base, 8), :] + apply(spread(state, keep), weights[side])
        return state

    lax.fori_loop(0, GROUPS // 2, pair, jnp.zeros((8, LANES), F32))


def backward_solve_kernel(packed, packed_b, vectors, states, out, even_g, odd_g, even_b, odd_b):
    weights_g, weights_b = (even_g, odd_g), (even_b, odd_b)
    row = lax.broadcasted_iota(jnp.int32, (8, LANES), 0)
    keep = kept()
    base = ROWS if vectors.shape[1] > 8 else 0
    last = GROUPS - 1

    def known(d, weights):
        vector = pltpu.roll(vectors[d, pl.ds(base, 8), :], COLS, 0)
        return vector + apply(spread(states[d], keep), weights)

    for e in range(2):
        unpack_matrix(packed, last - e, 0, weights_g[e])
    unpack_matrix(packed_b, last, 0, even_b)

    def pair(p, carry):
        end, ready = carry
        for side in range(2):
            e = 2 * p + side
            d = last - e
            out[d] = jnp.where(row < COLS, states[d], pltpu.roll(end, COLS, 0))
            after = jnp.maximum(d - 1, 0)
            following = known(after, weights_g[1 - side])
            unpack_matrix(packed, jnp.maximum(d - 2, 0), 0, weights_g[side])
            unpack_matrix(packed_b, after, 0, weights_b[1 - side])
            end = ready + apply(spread(end, keep), weights_b[side])
            ready = following
        return end, ready

    lax.fori_loop(0, GROUPS // 2, pair, (jnp.zeros((8, LANES), F32), known(last, even_g)))


def solve(kernel, slots, *arrays):
    return pl.pallas_call(
        kernel,
        out_shape=jax.ShapeDtypeStruct((GROUPS, 8, LANES), F32),
        in_specs=[whole()] * len(arrays),
        out_specs=whole(),
        scratch_shapes=[pltpu.VMEM((2 * LANES, 2 * LANES), BF16)] * slots,
        name=kernel.__name__,
        **params(8, 7),
    )(*arrays)


def exchange(value):
    return lax.all_to_all(value, "norm", 0, 0, tiled=True)


def shards(
    rhs, previous, minus_jac, plus_jac, dissipation, inverse_diag, lower_coupling, upper_coupling
):
    count = lax.axis_size("surf")
    up = [(i, (i + 1) % count) for i in range(count)]
    down = [((i + 1) % count, i) for i in range(count)]
    delta = previous
    low, high = edges(delta)
    backward_maps = backward_products(upper_coupling, low)
    forward_maps, chain = forward_products(lower_coupling, backward_maps)
    backward_maps = exchange(backward_maps.reshape(GROUPS, ROWS, LANES))
    forward_maps = forward_maps.reshape(GROUPS, FIRST, LANES)
    for sweep_index in range(SWEEPS):
        below = lax.ppermute(high, "surf", up)
        above = lax.ppermute(low, "surf", down)
        arrays = (
            rhs, delta, below, above, minus_jac, plus_jac, dissipation, inverse_diag, lower_coupling, upper_coupling
        )
        if sweep_index == 0:
            source, forward_maps = local_source(*arrays, packed=forward_maps)
            forward_maps = vectors = exchange(forward_maps)
            across_maps = exchange(backward_products(upper_coupling, source, chain).reshape(GROUPS, ROWS, LANES))
        else:
            source, vectors = local_source(*arrays)
            vectors = exchange(vectors)
        states = solve(forward_solve_kernel, 2, forward_maps, vectors)
        incoming = exchange(solve(backward_solve_kernel, 4, across_maps, backward_maps, vectors, states))
        last = sweep_index == SWEEPS - 1
        delta, *sides = finish(
            last, incoming.reshape(GROUPS * 8, LANES), source, lower_coupling, upper_coupling
        )
        if not last:
            low, high = sides
    return delta


def solution(mesh):
    line = P("norm", None, "surf")
    block = P("norm", None, None, "surf")
    return jax.shard_map(
        shards,
        mesh=mesh,
        in_specs=(line, line, block, block, line, block, block, block),
        out_specs=line,
        check_vma=False,
    )
```

```python
import functools

import jax
import jax.numpy as jnp
from jax import lax
from jax.experimental import pallas as pl
from jax.experimental.pallas import tpu as pltpu
from jax.sharding import PartitionSpec as P

SWEEPS = 2
N = 48
CELLS = 4
LANES = 128
MAT = N * N
GROUPS = 32
COLS = LANES // GROUPS
ROWS = 72
FIRST = ROWS + 8
ROOM = 60
F32 = jnp.float32
BF16 = jnp.bfloat16


def params(mebibytes, microseconds):
    cost = pl.CostEstimate(flops=int(microseconds * 1e9), bytes_accessed=0, transcendentals=0)
    return dict(
        compiler_params=pltpu.CompilerParams(vmem_limit_bytes=mebibytes * 1024 * 1024), cost_estimate=cost
    )


def whole():
    return pl.BlockSpec(memory_space=pltpu.VMEM)


def matmul_cells(left, right, out, add=None):
    def block(step, carry):
        base = pl.multiple_of(step * 4 * N, 8)
        sums = [None] * 4
        for b in range(N):
            vector = right[pl.ds(b * N, N), :]
            for k in range(4):
                term = left[pl.ds(base + k * N + b, 1), :] * vector
                sums[k] = term if sums[k] is None else sums[k] + term
        for k in range(4):
            where = pl.ds(pl.multiple_of(base + k * N, 8), N)
            value = sums[k]
            if add is not None:
                value = value + add[where, :]
            out[where, :] = value
        return carry

    lax.fori_loop(0, N // 4, block, 0)


def pack_matrix(mat, out, first):
    def column(c, lo, count):
        return mat[pl.ds(c + lo * N, count, stride=N), :]

    def main(r, carry):
        tile = jnp.concatenate(
            [column(r, 0, 48), column(32 + r, 0, 16), column(16 + r, 0, 48), column(32 + r, 16, 16)], axis=0
        ).T
        for i in range(COLS):
            for g in range(0, GROUPS, 8):
                out[pl.ds(g, 8), first + i * 16 + r, :] = tile[GROUPS * i + g : GROUPS * i + g + 8]
        return carry

    lax.fori_loop(0, 16, main, 0, unroll=4)

    def rest(r, carry):
        tile = jnp.concatenate(
            [column(32 + r, 32, 16), column(40 + r, 32, 16), jnp.zeros((96, LANES), F32)], axis=0
        ).T
        line = jnp.concatenate([tile[GROUPS * i : GROUPS * (i + 1), 0:32] for i in range(COLS)], axis=1)
        for g in range(0, GROUPS, 8):
            out[pl.ds(g, 8), first + 64 + r, :] = line[g : g + 8]
        return carry

    lax.fori_loop(0, 8, rest, 0, unroll=4)


def in_hbm():
    return pl.BlockSpec(memory_space=pltpu.HBM)


def widen(narrow, wide, copies, cells):
    for k in cells:
        copies[k].wait()

        def row(r, carry):
            wide[k, pl.ds(pl.multiple_of(r * N, 16), N), :] = narrow[k, r].astype(F32)
            return carry

        lax.fori_loop(0, N, row, 0, unroll=4)


def fetch(source, target, sems, order):
    copies = {k: pltpu.make_async_copy(source.at[k], target.at[k], sems.at[k]) for k in order}
    for k in order:
        copies[k].start()
    return copies


def write_out(packed, out, rows, sem):
    copy = pltpu.make_async_copy(packed, out.at[:, pl.ds(0, rows), :] if rows < out.shape[1] else out, sem)
    copy.start()
    copy.wait()


def forward_kernel(
    rhs, delta, below, above, minus, plus, dissipation, inverse, lower, upper, after,
    out, source, chain,
    narrow, low, work, packed, sems, chain_sems, out_sem, blocks, block_sems, hold, vectors,
):
    copies = fetch(lower, narrow, sems, (0, 1, 2, 3))
    others = [
        pltpu.make_async_copy(array, blocks.at[which], block_sems.at[which])
        for which, array in enumerate((minus, plus, inverse, upper))
    ]
    for copy in others:
        copy.start()
    kept = []

    def keep(k, ref):
        kept.append(pltpu.make_async_copy(ref, chain.at[k], chain_sems.at[k]))
        kept[-1].start()

    widen(narrow, low, copies, (0, 1))
    keep(0, low.at[0])
    for k in range(1, CELLS):
        before = low.at[0] if k == 1 else work.at[k - 2]
        if k > 1:
            widen(narrow, low, copies, (k,))
        matmul_cells(low.at[k], before, work.at[k - 1])
        keep(k, work.at[k - 1])
    pack_matrix(work.at[CELLS - 2], packed, 0)
    copy = pltpu.make_async_copy(packed, out.at[:, pl.ds(0, ROWS), :], out_sem)
    copy.start()
    for other in others:
        other.wait()
    source_kernel(
        rhs, delta, below, above, blocks.at[0], blocks.at[1], dissipation, blocks.at[2], narrow, blocks.at[3],
        source, vectors, hold,
    )
    copy.wait()
    copy = pltpu.make_async_copy(vectors, out.at[:, pl.ds(ROWS, 8), :], out_sem)
    copy.start()
    copy.wait()
    for copy in kept:
        copy.wait()


def product_scratch(works):
    return [
        pltpu.VMEM((CELLS, N, N, LANES), BF16),
        pltpu.VMEM((CELLS, MAT, LANES), F32),
        pltpu.VMEM((works, MAT, LANES), F32),
        pltpu.VMEM((GROUPS, ROWS, LANES), F32),
        pltpu.SemaphoreType.DMA((CELLS,)),
        pltpu.SemaphoreType.DMA((CELLS,)),
        pltpu.SemaphoreType.DMA,
    ]


def forward_products(*arrays):
    lines = (CELLS, N, LANES)
    return pl.pallas_call(
        forward_kernel,
        out_shape=(
            jax.ShapeDtypeStruct((GROUPS, FIRST, LANES), F32),
            jax.ShapeDtypeStruct(lines, F32),
            jax.ShapeDtypeStruct((CELLS, MAT, LANES), F32),
        ),
        in_specs=[whole()] * 4 + [in_hbm()] * 2 + [whole()] + [in_hbm()] * 4,
        out_specs=(in_hbm(), whole(), in_hbm()),
        scratch_shapes=product_scratch(3)
        + [
            pltpu.VMEM((4, CELLS, N, N, LANES), BF16),
            pltpu.SemaphoreType.DMA((4,)),
            pltpu.VMEM(lines, F32),
            pltpu.VMEM((GROUPS, 8, LANES), F32),
        ],
        name="forward_products",
        **params(ROOM - 5, 17),
    )(*arrays)


def backward_kernel(upper, after, out, narrow, upp, work, packed, sems, more_sems, out_sem):
    copies = fetch(upper, narrow, sems, (3, 2, 1, 0))
    widen(narrow, upp, copies, (3, 2))
    matmul_cells(upp.at[2], upp.at[3], work.at[0])
    widen(narrow, upp, copies, (1,))
    matmul_cells(upp.at[1], work.at[0], work.at[1])
    widen(narrow, upp, copies, (0,))
    matmul_cells(upp.at[0], work.at[1], work.at[0])
    pack_matrix(work.at[0], packed, 0)
    write_out(packed, out, ROWS, out_sem)


def across_kernel(upper, after, chain, out, narrow, upp, work, packed, sems, chain_sems, out_sem, have):
    copies = fetch(upper, narrow, sems, (2,))
    chains = fetch(chain, have, chain_sems, (3, 2, 1, 0))
    copies.update(fetch(upper, narrow, sems, (1, 0)))
    widen(narrow, upp, copies, (2,))
    chains[3].wait()
    chains[2].wait()
    matmul_cells(upp.at[2], have.at[3], work.at[0], have.at[2])
    widen(narrow, upp, copies, (1,))
    chains[1].wait()
    matmul_cells(upp.at[1], work.at[0], work.at[1], have.at[1])
    widen(narrow, upp, copies, (0,))
    chains[0].wait()
    matmul_cells(upp.at[0], work.at[1], work.at[0], have.at[0])
    pack_matrix(work.at[0], packed, 0)
    write_out(packed, out, ROWS, out_sem)


def backward_products(upper, after, chain=None):
    across = chain is not None
    return pl.pallas_call(
        across_kernel if across else backward_kernel,
        out_shape=jax.ShapeDtypeStruct((GROUPS, ROWS, LANES), F32),
        in_specs=[in_hbm()] * (3 if across else 2),
        out_specs=in_hbm(),
        scratch_shapes=product_scratch(2) + [pltpu.VMEM((CELLS, MAT, LANES), F32)] * across,
        name="across_products" if across else "backward_products",
        **params(ROOM, 15),
    )(*((upper, after, chain) if across else (upper, after)))


def fold(parts):
    row = lax.broadcasted_iota(jnp.int32, (8, LANES), 0)
    for width in (4, 2, 1):
        lower_half = (row & width) == 0
        parts = [
            jnp.where(lower_half, one, two)
            + jnp.where(lower_half, pltpu.roll(one, 8 - width, 0), pltpu.roll(two, width, 0))
            for one, two in zip(parts[:width], parts[width:])
        ]
    return parts[0]


def matvec(block, vector):
    tiles = []
    for first in range(0, N, 8):
        parts = []
        for a in range(first, first + 8):
            product = block[a].astype(F32) * vector
            parts.append(sum(product[b : b + 8] for b in range(8, N, 8)) + product[0:8])
        tiles.append(fold(parts))
    return jnp.concatenate(tiles, axis=0)


def write_edges(delta, low, high):
    gap = jnp.zeros((LANES - 2 * N, LANES), F32)
    tiles = [jnp.concatenate([delta[2 * p], delta[2 * p + 1], gap], axis=0).T for p in range(2)]
    empty = jnp.zeros((4, LANES), F32)
    low[...] = jnp.concatenate([tiles[0][0:2], tiles[1][0:2], empty], axis=0)
    high[...] = jnp.concatenate([tiles[0][LANES - 2 :], tiles[1][LANES - 2 :], empty], axis=0)


def edges(delta):
    return pl.pallas_call(
        write_edges,
        out_shape=(jax.ShapeDtypeStruct((8, LANES), F32),) * 2,
        in_specs=[whole()],
        out_specs=(whole(),) * 2,
        name="edges",
        **params(4, 1),
    )(delta)


def source_kernel(
    rhs, delta, below, above, minus, plus, dissipation, inverse, lower, upper,
    source, vectors, hold,
):
    lane = lax.broadcasted_iota(jnp.int32, (N, LANES), 1)
    place = lax.axis_index("surf")
    gap = jnp.zeros((LANES - 8, LANES), F32)
    before = jnp.concatenate([jnp.where(place == 0, 0.0, below[...]), gap], axis=0).T
    after = jnp.concatenate([jnp.where(place == lax.axis_size("surf") - 1, 0.0, above[...]), gap], axis=0).T
    forward = jnp.zeros((N, LANES), F32)
    for k in range(CELLS):
        centre = delta[k]
        first = k // 2 * 2
        left = before[k % 2 * N : k % 2 * N + N]
        right = after[k % 2 * N : k % 2 * N + N]

        def shifted(by):
            here = pltpu.roll(centre, by % LANES, 1)
            if by > 0:
                return jnp.where(lane < by, pltpu.roll(left, (by - 2 - first) % LANES, 1), here)
            return jnp.where(lane >= LANES + by, pltpu.roll(right, (by - first) % LANES, 1), here)

        left_one, right_one = shifted(1), shifted(-1)
        fourth = shifted(2) - 4.0 * left_one + 6.0 * centre - 4.0 * right_one + shifted(-2)
        residual = rhs[k] - dissipation[k] * fourth
        residual = residual - matvec(minus.at[k], left_one) - matvec(plus.at[k], right_one)
        value = matvec(inverse.at[k], residual)
        source[k] = value
        forward = value + matvec(lower.at[k], forward) if k else value
        hold[k] = forward
    backward = hold[CELLS - 1]
    for k in range(CELLS - 2, -1, -1):
        backward = hold[k] + matvec(upper.at[k], backward)
    gap = jnp.zeros((16, LANES), F32)
    for row, value in ((0, forward), (COLS, backward)):
        tile = jnp.concatenate([value, gap, value, gap], axis=0).T
        for i in range(COLS):
            for g in range(0, GROUPS, 8):
                start = GROUPS * i + g
                vectors[pl.ds(g, 8), row + i, :] = tile[start : start + 8]


def local_source(*arrays):
    lines = (CELLS, N, LANES)
    return pl.pallas_call(
        source_kernel,
        out_shape=(jax.ShapeDtypeStruct(lines, F32), jax.ShapeDtypeStruct((GROUPS, 8, LANES), F32)),
        in_specs=[whole()] * 10,
        out_specs=(whole(), whole()),
        scratch_shapes=[pltpu.VMEM(lines, F32)],
        name="local_source",
        **params(16, 3),
    )(*arrays)


def finish_kernel(incoming, source, lower, upper, delta, *rest):
    hold = rest[-1]

    def incoming_line(row):
        rows = [incoming[pl.ds(row + i, GROUPS, stride=8), :] for i in range(COLS)]
        return jnp.concatenate(rows, axis=0).T[0:N]

    value = incoming_line(0)
    for k in range(CELLS):
        value = source[k] + matvec(lower.at[k], value)
        hold[k] = value
    value = incoming_line(COLS)
    for k in range(CELLS - 1, -1, -1):
        value = hold[k] + matvec(upper.at[k], value)
        delta[k] = value
    if len(rest) > 1:
        write_edges(delta, rest[0], rest[1])


def finish(last, *arrays):
    edge = jax.ShapeDtypeStruct((8, LANES), F32)
    results = (jax.ShapeDtypeStruct((CELLS, N, LANES), F32),) + (() if last else (edge, edge))
    return pl.pallas_call(
        finish_kernel,
        out_shape=results,
        in_specs=[whole()] * 4,
        out_specs=(whole(),) * len(results),
        scratch_shapes=[pltpu.VMEM((CELLS, N, LANES), F32)],
        name="finish",
        **params(8, 1.5),
    )(*arrays)


def split(value):
    high = value.astype(BF16)
    return high, (value - high.astype(F32)).astype(BF16)


def unpack_matrix(packed, d, first, weights):
    lane = lax.broadcasted_iota(jnp.int32, (16, LANES), 1)
    extra = packed[d, pl.ds(first + 64, 8), :]
    for i in range(COLS):
        block = packed[d, pl.ds(first + 16 * i, 16), :]
        turned = pltpu.roll(block, 64, 1)
        low = jnp.where(lane < 64, block, turned)
        high = jnp.where(lane < 64, turned, block)
        tail = jnp.concatenate(
            [pltpu.roll(extra, (32 - 32 * i) % LANES, 1), pltpu.roll(extra, (16 - 32 * i) % LANES, 1)], axis=0
        )
        third = jnp.where(lane < 16, pltpu.roll(block, 80, 1), jnp.where(lane < 32, pltpu.roll(block, 32, 1), tail))
        third = jnp.where(lane < 64, third, pltpu.roll(third, 64, 1))
        both = jnp.concatenate([low, high, third], axis=0)
        first_part, second_part = split(both)
        weights[pl.ds(64 * i, N), 0:LANES] = first_part
        weights[pl.ds(64 * i, N), LANES : 2 * LANES] = second_part


def clear_gaps(*weights):
    for ref in weights:
        for i in range(COLS):
            ref[pl.ds(64 * i + N, 64 - N), :] = jnp.zeros((64 - N, 2 * LANES), BF16)


def spread(value, keep):
    wide = jnp.where(keep, jnp.concatenate([value, value], axis=1), 0.0)
    high = wide.astype(BF16).astype(F32)
    return jnp.concatenate([high, wide - high], axis=0).astype(BF16)


def kept():
    row = lax.broadcasted_iota(jnp.int32, (8, 2 * LANES), 0)
    lane = lax.broadcasted_iota(jnp.int32, (8, 2 * LANES), 1)
    return jnp.logical_and(row == lane // 64, lax.rem(lane, 64) < N)


def apply(left, weights):
    out = jnp.dot(left, weights[...], preferred_element_type=F32)
    return (out[0:8, 0:LANES] + out[8:16, 0:LANES]) + (out[0:8, LANES:] + out[8:16, LANES:])


def forward_solve_kernel(packed, vectors, out, even, odd):
    weights = (even, odd)
    keep = kept()
    base = ROWS if vectors.shape[1] > 8 else 0
    clear_gaps(even, odd)
    unpack_matrix(packed, 0, 0, even)

    def pair(e, state):
        for side in range(2):
            d = 2 * e + side
            product = apply(spread(state, keep), weights[side])
            vector = vectors[d, pl.ds(base, 8), :]
            out[d, 0:8] = state
            out[d, 8:16] = vector
            unpack_matrix(packed, jnp.minimum(d + 1, GROUPS - 1), 0, weights[1 - side])
            state = vector + product
        return state

    lax.fori_loop(0, GROUPS // 2, pair, jnp.zeros((8, LANES), F32))


def backward_solve_kernel(packed, packed_b, states, out, even_g, odd_g, even_b, odd_b):
    weights_g, weights_b = (even_g, odd_g), (even_b, odd_b)
    row = lax.broadcasted_iota(jnp.int32, (8, LANES), 0)
    keep = kept()
    last = GROUPS - 1

    def known(d, weights):
        vector = pltpu.roll(states[d, 8:16], COLS, 0)
        return vector + apply(spread(states[d, 0:8], keep), weights)

    clear_gaps(even_g, odd_g, even_b, odd_b)
    for e in range(2):
        unpack_matrix(packed, last - e, 0, weights_g[e])
    unpack_matrix(packed_b, last, 0, even_b)

    def pair(p, carry):
        end, ready = carry
        for side in range(2):
            e = 2 * p + side
            d = last - e
            product = apply(spread(end, keep), weights_b[side])
            out[d] = jnp.where(row < COLS, states[d, 0:8], pltpu.roll(end, COLS, 0))
            after = jnp.maximum(d - 1, 0)
            end = ready + product
            ready = known(after, weights_g[1 - side])
            unpack_matrix(packed_b, after, 0, weights_b[1 - side])
            unpack_matrix(packed, jnp.maximum(d - 2, 0), 0, weights_g[side])
        return end, ready

    lax.fori_loop(0, GROUPS // 2, pair, (jnp.zeros((8, LANES), F32), known(last, even_g)))


def solve(kernel, slots, rows, room, *arrays):
    return pl.pallas_call(
        kernel,
        out_shape=jax.ShapeDtypeStruct((GROUPS, rows, LANES), F32),
        in_specs=[whole()] * len(arrays),
        out_specs=whole(),
        scratch_shapes=[pltpu.VMEM((2 * LANES, 2 * LANES), BF16)] * slots,
        name=kernel.__name__,
        **params(room, 7),
    )(*arrays)


def exchange(value):
    return lax.all_to_all(value, "norm", 0, 0, tiled=True)


def shards(
    rhs, previous, minus_jac, plus_jac, dissipation, inverse_diag, lower_coupling, upper_coupling
):
    count = lax.axis_size("surf")
    up = [(i, (i + 1) % count) for i in range(count)]
    down = [((i + 1) % count, i) for i in range(count)]
    delta = previous
    low, high = edges(delta)
    backward_maps = backward_products(upper_coupling, low)
    for sweep_index in range(SWEEPS):
        below = lax.ppermute(high, "surf", up)
        above = lax.ppermute(low, "surf", down)
        arrays = (
            rhs, delta, below, above, minus_jac, plus_jac, dissipation, inverse_diag, lower_coupling, upper_coupling
        )
        room = ROOM if sweep_index == 0 else 8
        if sweep_index == 0:
            forward_maps, source, chain = forward_products(*arrays, backward_maps)
            backward_maps = exchange(backward_maps)
            across_maps = backward_products(upper_coupling, forward_maps, chain)
            forward_maps = vectors = exchange(forward_maps)
            across_maps = exchange(across_maps)
        else:
            source, vectors = local_source(*arrays)
            vectors = exchange(vectors)
        states = solve(forward_solve_kernel, 2, 16, room, forward_maps, vectors)
        incoming = exchange(solve(backward_solve_kernel, 4, 8, 8, across_maps, backward_maps, states))
        last = sweep_index == SWEEPS - 1
        delta, *sides = finish(
            last, incoming.reshape(GROUPS * 8, LANES), source, lower_coupling, upper_coupling
        )
        if not last:
            low, high = sides
    return delta


def solution(mesh):
    line = P("norm", None, "surf")
    block = P("norm", None, None, "surf")
    return jax.shard_map(
        shards,
        mesh=mesh,
        in_specs=(line, line, block, block, line, block, block, block),
        out_specs=line,
        check_vma=False,
    )
```

```python
import functools

import jax
import jax.numpy as jnp
from jax import lax
from jax.experimental import pallas as pl
from jax.experimental.pallas import tpu as pltpu
from jax.sharding import PartitionSpec as P

SWEEPS = 2
N = 48
CELLS = 4
LANES = 128
MAT = N * N
GROUPS = 32
COLS = LANES // GROUPS
ROWS = 72
FIRST = ROWS + 8
ROOM = 60
F32 = jnp.float32
BF16 = jnp.bfloat16


def params(mebibytes, microseconds):
    cost = pl.CostEstimate(flops=int(microseconds * 1e9), bytes_accessed=0, transcendentals=0)
    return dict(
        compiler_params=pltpu.CompilerParams(vmem_limit_bytes=mebibytes * 1024 * 1024), cost_estimate=cost
    )


def whole():
    return pl.BlockSpec(memory_space=pltpu.VMEM)


def matmul_cells(left, right, out, add=None):
    def block(step, carry):
        base = pl.multiple_of(step * 4 * N, 8)
        sums = [None] * 4
        for b in range(N):
            vector = right[pl.ds(b * N, N), :]
            for k in range(4):
                term = left[pl.ds(base + k * N + b, 1), :] * vector
                sums[k] = term if sums[k] is None else sums[k] + term
        for k in range(4):
            where = pl.ds(pl.multiple_of(base + k * N, 8), N)
            value = sums[k]
            if add is not None:
                value = value + add[where, :]
            out[where, :] = value
        return carry

    lax.fori_loop(0, N // 4, block, 0)


def pack_matrix(mat, out, first):
    def column(c, lo, count):
        return mat[pl.ds(c + lo * N, count, stride=N), :]

    def main(r, carry):
        tile = jnp.concatenate(
            [column(r, 0, 48), column(32 + r, 0, 16), column(16 + r, 0, 48), column(32 + r, 16, 16)], axis=0
        ).T
        for i in range(COLS):
            for g in range(0, GROUPS, 8):
                out[pl.ds(g, 8), first + i * 16 + r, :] = tile[GROUPS * i + g : GROUPS * i + g + 8]
        return carry

    lax.fori_loop(0, 16, main, 0, unroll=4)

    def rest(r, carry):
        tile = jnp.concatenate(
            [column(32 + r, 32, 16), column(40 + r, 32, 16), jnp.zeros((96, LANES), F32)], axis=0
        ).T
        line = jnp.concatenate([tile[GROUPS * i : GROUPS * (i + 1), 0:32] for i in range(COLS)], axis=1)
        for g in range(0, GROUPS, 8):
            out[pl.ds(g, 8), first + 64 + r, :] = line[g : g + 8]
        return carry

    lax.fori_loop(0, 8, rest, 0, unroll=4)


def in_hbm():
    return pl.BlockSpec(memory_space=pltpu.HBM)


def widen(narrow, wide, copies, cells):
    for k in cells:
        copies[k].wait()

        def row(r, carry):
            wide[k, pl.ds(pl.multiple_of(r * N, 16), N), :] = narrow[k, r].astype(F32)
            return carry

        lax.fori_loop(0, N, row, 0, unroll=4)


def fetch(source, target, sems, order):
    copies = {k: pltpu.make_async_copy(source.at[k], target.at[k], sems.at[k]) for k in order}
    for k in order:
        copies[k].start()
    return copies


def write_out(packed, out, rows, sem):
    copy = pltpu.make_async_copy(packed, out.at[:, pl.ds(0, rows), :] if rows < out.shape[1] else out, sem)
    copy.start()
    copy.wait()


def forward_kernel(
    rhs, delta, below, above, minus, plus, dissipation, inverse, lower, upper, after,
    out, source, chain,
    narrow, low, work, packed, sems, chain_sems, out_sem, blocks, block_sems, hold, vectors,
):
    copies = fetch(lower, narrow, sems, (0, 1, 2, 3))
    others = [
        pltpu.make_async_copy(array, blocks.at[which], block_sems.at[which])
        for which, array in enumerate((minus, plus, inverse, upper))
    ]
    for copy in others:
        copy.start()
    kept = []

    def keep(k, ref):
        kept.append(pltpu.make_async_copy(ref, chain.at[k], chain_sems.at[k]))
        kept[-1].start()

    widen(narrow, low, copies, (0, 1))
    keep(0, low.at[0])
    for k in range(1, CELLS):
        before = low.at[0] if k == 1 else work.at[k - 2]
        if k > 1:
            widen(narrow, low, copies, (k,))
        matmul_cells(low.at[k], before, work.at[k - 1])
        keep(k, work.at[k - 1])
    pack_matrix(work.at[CELLS - 2], packed, 0)
    copy = pltpu.make_async_copy(packed, out.at[:, pl.ds(0, ROWS), :], out_sem)
    copy.start()
    for other in others:
        other.wait()
    source_kernel(
        rhs, delta, below, above, blocks.at[0], blocks.at[1], dissipation, blocks.at[2], narrow, blocks.at[3],
        source, vectors, hold,
    )
    copy.wait()
    copy = pltpu.make_async_copy(vectors, out.at[:, pl.ds(ROWS, 8), :], out_sem)
    copy.start()
    copy.wait()
    for copy in kept:
        copy.wait()


def product_scratch(works):
    return [
        pltpu.VMEM((CELLS, N, N, LANES), BF16),
        pltpu.VMEM((CELLS, MAT, LANES), F32),
        pltpu.VMEM((works, MAT, LANES), F32),
        pltpu.VMEM((GROUPS, ROWS, LANES), F32),
        pltpu.SemaphoreType.DMA((CELLS,)),
        pltpu.SemaphoreType.DMA((CELLS,)),
        pltpu.SemaphoreType.DMA,
    ]


def forward_products(*arrays):
    lines = (CELLS, N, LANES)
    return pl.pallas_call(
        forward_kernel,
        out_shape=(
            jax.ShapeDtypeStruct((GROUPS, FIRST, LANES), F32),
            jax.ShapeDtypeStruct(lines, F32),
            jax.ShapeDtypeStruct((CELLS, MAT, LANES), F32),
        ),
        in_specs=[whole()] * 4 + [in_hbm()] * 2 + [whole()] + [in_hbm()] * 4,
        out_specs=(in_hbm(), whole(), in_hbm()),
        scratch_shapes=product_scratch(3)
        + [
            pltpu.VMEM((4, CELLS, N, N, LANES), BF16),
            pltpu.SemaphoreType.DMA((4,)),
            pltpu.VMEM(lines, F32),
            pltpu.VMEM((GROUPS, 8, LANES), F32),
        ],
        name="forward_products",
        **params(ROOM - 8, 17),
    )(*arrays)


def backward_kernel(upper, after, out, narrow, upp, work, packed, sems, more_sems, out_sem):
    copies = fetch(upper, narrow, sems, (3, 2, 1, 0))
    widen(narrow, upp, copies, (3, 2))
    matmul_cells(upp.at[2], upp.at[3], work.at[0])
    widen(narrow, upp, copies, (1,))
    matmul_cells(upp.at[1], work.at[0], work.at[1])
    widen(narrow, upp, copies, (0,))
    matmul_cells(upp.at[0], work.at[1], work.at[0])
    pack_matrix(work.at[0], packed, 0)
    write_out(packed, out, ROWS, out_sem)


def across_kernel(upper, after, chain, out, narrow, upp, work, packed, sems, chain_sems, out_sem, have):
    copies = fetch(upper, narrow, sems, (2,))
    chains = fetch(chain, have, chain_sems, (3, 2, 1, 0))
    copies.update(fetch(upper, narrow, sems, (1, 0)))
    widen(narrow, upp, copies, (2,))
    chains[3].wait()
    chains[2].wait()
    matmul_cells(upp.at[2], have.at[3], work.at[0], have.at[2])
    widen(narrow, upp, copies, (1,))
    chains[1].wait()
    matmul_cells(upp.at[1], work.at[0], work.at[1], have.at[1])
    widen(narrow, upp, copies, (0,))
    chains[0].wait()
    matmul_cells(upp.at[0], work.at[1], work.at[0], have.at[0])
    pack_matrix(work.at[0], packed, 0)
    write_out(packed, out, ROWS, out_sem)


def backward_products(upper, after, chain=None):
    across = chain is not None
    return pl.pallas_call(
        across_kernel if across else backward_kernel,
        out_shape=jax.ShapeDtypeStruct((GROUPS, ROWS, LANES), F32),
        in_specs=[in_hbm()] * (3 if across else 2),
        out_specs=in_hbm(),
        scratch_shapes=product_scratch(2) + [pltpu.VMEM((CELLS, MAT, LANES), F32)] * across,
        name="across_products" if across else "backward_products",
        **params(ROOM, 15),
    )(*((upper, after, chain) if across else (upper, after)))


def fold(parts):
    row = lax.broadcasted_iota(jnp.int32, (8, LANES), 0)
    for width in (4, 2, 1):
        lower_half = (row & width) == 0
        parts = [
            jnp.where(lower_half, one, two)
            + jnp.where(lower_half, pltpu.roll(one, 8 - width, 0), pltpu.roll(two, width, 0))
            for one, two in zip(parts[:width], parts[width:])
        ]
    return parts[0]


def matvec(block, vector):
    tiles = []
    for first in range(0, N, 8):
        parts = []
        for a in range(first, first + 8):
            product = block[a].astype(F32) * vector
            parts.append(sum(product[b : b + 8] for b in range(8, N, 8)) + product[0:8])
        tiles.append(fold(parts))
    return jnp.concatenate(tiles, axis=0)


def write_edges(delta, low, high):
    gap = jnp.zeros((LANES - 2 * N, LANES), F32)
    tiles = [jnp.concatenate([delta[2 * p], delta[2 * p + 1], gap], axis=0).T for p in range(2)]
    empty = jnp.zeros((4, LANES), F32)
    low[...] = jnp.concatenate([tiles[0][0:2], tiles[1][0:2], empty], axis=0)
    high[...] = jnp.concatenate([tiles[0][LANES - 2 :], tiles[1][LANES - 2 :], empty], axis=0)


def edges(delta):
    return pl.pallas_call(
        write_edges,
        out_shape=(jax.ShapeDtypeStruct((8, LANES), F32),) * 2,
        in_specs=[whole()],
        out_specs=(whole(),) * 2,
        name="edges",
        **params(4, 1),
    )(delta)


def source_kernel(
    rhs, delta, below, above, minus, plus, dissipation, inverse, lower, upper,
    source, vectors, hold,
):
    lane = lax.broadcasted_iota(jnp.int32, (N, LANES), 1)
    place = lax.axis_index("surf")
    gap = jnp.zeros((LANES - 8, LANES), F32)
    before = jnp.concatenate([jnp.where(place == 0, 0.0, below[...]), gap], axis=0).T
    after = jnp.concatenate([jnp.where(place == lax.axis_size("surf") - 1, 0.0, above[...]), gap], axis=0).T
    forward = jnp.zeros((N, LANES), F32)
    for k in range(CELLS):
        centre = delta[k]
        first = k // 2 * 2
        left = before[k % 2 * N : k % 2 * N + N]
        right = after[k % 2 * N : k % 2 * N + N]

        def shifted(by):
            here = pltpu.roll(centre, by % LANES, 1)
            if by > 0:
                return jnp.where(lane < by, pltpu.roll(left, (by - 2 - first) % LANES, 1), here)
            return jnp.where(lane >= LANES + by, pltpu.roll(right, (by - first) % LANES, 1), here)

        left_one, right_one = shifted(1), shifted(-1)
        fourth = shifted(2) - 4.0 * left_one + 6.0 * centre - 4.0 * right_one + shifted(-2)
        residual = rhs[k] - dissipation[k] * fourth
        residual = residual - matvec(minus.at[k], left_one) - matvec(plus.at[k], right_one)
        value = matvec(inverse.at[k], residual)
        source[k] = value
        forward = value + matvec(lower.at[k], forward) if k else value
        hold[k] = forward
    backward = hold[CELLS - 1]
    for k in range(CELLS - 2, -1, -1):
        backward = hold[k] + matvec(upper.at[k], backward)
    gap = jnp.zeros((16, LANES), F32)
    for row, value in ((0, forward), (COLS, backward)):
        tile = jnp.concatenate([value, gap, value, gap], axis=0).T
        for i in range(COLS):
            for g in range(0, GROUPS, 8):
                start = GROUPS * i + g
                vectors[pl.ds(g, 8), row + i, :] = tile[start : start + 8]


def local_source(*arrays):
    lines = (CELLS, N, LANES)
    return pl.pallas_call(
        source_kernel,
        out_shape=(jax.ShapeDtypeStruct(lines, F32), jax.ShapeDtypeStruct((GROUPS, 8, LANES), F32)),
        in_specs=[whole()] * 10,
        out_specs=(whole(), whole()),
        scratch_shapes=[pltpu.VMEM(lines, F32)],
        name="local_source",
        **params(16, 3),
    )(*arrays)


def finish_kernel(incoming, source, lower, upper, delta, *rest):
    hold = rest[-1]

    def incoming_line(row):
        rows = [incoming[pl.ds(row + i, GROUPS, stride=8), :] for i in range(COLS)]
        return jnp.concatenate(rows, axis=0).T[0:N]

    value = incoming_line(0)
    for k in range(CELLS):
        value = source[k] + matvec(lower.at[k], value)
        hold[k] = value
    value = incoming_line(COLS)
    for k in range(CELLS - 1, -1, -1):
        value = hold[k] + matvec(upper.at[k], value)
        delta[k] = value
    if len(rest) > 1:
        write_edges(delta, rest[0], rest[1])


def finish(last, *arrays):
    edge = jax.ShapeDtypeStruct((8, LANES), F32)
    results = (jax.ShapeDtypeStruct((CELLS, N, LANES), F32),) + (() if last else (edge, edge))
    return pl.pallas_call(
        finish_kernel,
        out_shape=results,
        in_specs=[whole()] * 4,
        out_specs=(whole(),) * len(results),
        scratch_shapes=[pltpu.VMEM((CELLS, N, LANES), F32)],
        name="finish",
        **params(8, 1.5),
    )(*arrays)


def split(value):
    high = value.astype(BF16)
    return high, (value - high.astype(F32)).astype(BF16)


def unpack_matrix(packed, d, first, weights):
    lane = lax.broadcasted_iota(jnp.int32, (16, LANES), 1)
    extra = packed[d, pl.ds(first + 64, 8), :]
    for i in range(COLS):
        block = packed[d, pl.ds(first + 16 * i, 16), :]
        turned = pltpu.roll(block, 64, 1)
        low = jnp.where(lane < 64, block, turned)
        high = jnp.where(lane < 64, turned, block)
        tail = jnp.concatenate(
            [pltpu.roll(extra, (32 - 32 * i) % LANES, 1), pltpu.roll(extra, (16 - 32 * i) % LANES, 1)], axis=0
        )
        third = jnp.where(lane < 16, pltpu.roll(block, 80, 1), jnp.where(lane < 32, pltpu.roll(block, 32, 1), tail))
        third = jnp.where(lane < 64, third, pltpu.roll(third, 64, 1))
        both = jnp.concatenate([low, high, third], axis=0)
        first_part, second_part = split(both)
        weights[pl.ds(64 * i, N), 0:LANES] = first_part
        weights[pl.ds(64 * i, N), LANES : 2 * LANES] = second_part


def clear_gaps(*weights):
    for ref in weights:
        for i in range(COLS):
            ref[pl.ds(64 * i + N, 64 - N), :] = jnp.zeros((64 - N, 2 * LANES), BF16)


def spread(value, keep):
    wide = jnp.where(keep, jnp.concatenate([value, value], axis=1), 0.0)
    high = wide.astype(BF16).astype(F32)
    return jnp.concatenate([high, wide - high], axis=0).astype(BF16)


def kept():
    row = lax.broadcasted_iota(jnp.int32, (8, 2 * LANES), 0)
    lane = lax.broadcasted_iota(jnp.int32, (8, 2 * LANES), 1)
    return jnp.logical_and(row == lane // 64, lax.rem(lane, 64) < N)


def apply(left, weights):
    out = jnp.dot(left, weights[...], preferred_element_type=F32)
    return (out[0:8, 0:LANES] + out[8:16, 0:LANES]) + (out[0:8, LANES:] + out[8:16, LANES:])


def forward_solve_kernel(packed, vectors, out, even, odd):
    weights = (even, odd)
    keep = kept()
    base = ROWS if vectors.shape[1] > 8 else 0
    clear_gaps(even, odd)
    unpack_matrix(packed, 0, 0, even)

    def pair(e, state):
        for side in range(2):
            d = 2 * e + side
            product = apply(spread(state, keep), weights[side])
            vector = vectors[d, pl.ds(base, 8), :]
            out[d, 0:8] = state
            out[d, 8:16] = vector
            unpack_matrix(packed, jnp.minimum(d + 1, GROUPS - 1), 0, weights[1 - side])
            state = vector + product
        return state

    lax.fori_loop(0, GROUPS // 2, pair, jnp.zeros((8, LANES), F32))


def backward_solve_kernel(packed, packed_b, states, out, even_g, odd_g, even_b, odd_b):
    weights_g, weights_b = (even_g, odd_g), (even_b, odd_b)
    row = lax.broadcasted_iota(jnp.int32, (8, LANES), 0)
    keep = kept()
    last = GROUPS - 1

    def known(d, weights):
        vector = pltpu.roll(states[d, 8:16], COLS, 0)
        return vector + apply(spread(states[d, 0:8], keep), weights)

    clear_gaps(even_g, odd_g, even_b, odd_b)
    for e in range(2):
        unpack_matrix(packed, last - e, 0, weights_g[e])
    unpack_matrix(packed_b, last, 0, even_b)

    def pair(p, carry):
        end, ready = carry
        for side in range(2):
            e = 2 * p + side
            d = last - e
            product = apply(spread(end, keep), weights_b[side])
            out[d] = jnp.where(row < COLS, states[d, 0:8], pltpu.roll(end, COLS, 0))
            after = jnp.maximum(d - 1, 0)
            end = ready + product
            ready = known(after, weights_g[1 - side])
            unpack_matrix(packed_b, after, 0, weights_b[1 - side])
            unpack_matrix(packed, jnp.maximum(d - 2, 0), 0, weights_g[side])
        return end, ready

    lax.fori_loop(0, GROUPS // 2, pair, (jnp.zeros((8, LANES), F32), known(last, even_g)))


def solve_kernel(packed, vectors, across, packed_b, out, *rest):
    *weights, states, held, sem = rest
    copy = pltpu.make_async_copy(across, held, sem)
    copy.start()
    forward_solve_kernel(packed, vectors, states, *weights[:2])
    copy.wait()
    backward_solve_kernel(held, packed_b, states, out, *weights[2:])


def solve_both(*arrays):
    return pl.pallas_call(
        solve_kernel,
        out_shape=jax.ShapeDtypeStruct((GROUPS, 8, LANES), F32),
        in_specs=[whole(), whole(), in_hbm(), whole()],
        out_specs=whole(),
        scratch_shapes=[pltpu.VMEM((2 * LANES, 2 * LANES), BF16)] * 6
        + [
            pltpu.VMEM((GROUPS, 16, LANES), F32),
            pltpu.VMEM((GROUPS, ROWS, LANES), F32),
            pltpu.SemaphoreType.DMA,
        ],
        name="solve_both",
        **params(12, 12),
    )(*arrays)


def solve(kernel, slots, rows, room, *arrays):
    return pl.pallas_call(
        kernel,
        out_shape=jax.ShapeDtypeStruct((GROUPS, rows, LANES), F32),
        in_specs=[whole()] * len(arrays),
        out_specs=whole(),
        scratch_shapes=[pltpu.VMEM((2 * LANES, 2 * LANES), BF16)] * slots,
        name=kernel.__name__,
        **params(room, 7),
    )(*arrays)


def exchange(value):
    return lax.all_to_all(value, "norm", 0, 0, tiled=True)


def shards(
    rhs, previous, minus_jac, plus_jac, dissipation, inverse_diag, lower_coupling, upper_coupling
):
    count = lax.axis_size("surf")
    up = [(i, (i + 1) % count) for i in range(count)]
    down = [((i + 1) % count, i) for i in range(count)]
    delta = previous
    low, high = edges(delta)
    backward_maps = backward_products(upper_coupling, low)
    for sweep_index in range(SWEEPS):
        below = lax.ppermute(high, "surf", up)
        above = lax.ppermute(low, "surf", down)
        arrays = (
            rhs, delta, below, above, minus_jac, plus_jac, dissipation, inverse_diag, lower_coupling, upper_coupling
        )
        if sweep_index == 0:
            forward_maps, source, chain = forward_products(*arrays, backward_maps)
            backward_maps = exchange(backward_maps)
            across_maps = backward_products(upper_coupling, forward_maps, chain)
            forward_maps = vectors = exchange(forward_maps)
            across_maps = exchange(across_maps)
        else:
            source, vectors = local_source(*arrays)
            vectors = exchange(vectors)
        if sweep_index == 0:
            states = solve(forward_solve_kernel, 2, 16, ROOM, forward_maps, vectors)
            incoming = solve(backward_solve_kernel, 4, 8, 8, across_maps, backward_maps, states)
        else:
            incoming = solve_both(forward_maps, vectors, across_maps, backward_maps)
        incoming = exchange(incoming)
        last = sweep_index == SWEEPS - 1
        delta, *sides = finish(
            last, incoming.reshape(GROUPS * 8, LANES), source, lower_coupling, upper_coupling
        )
        if not last:
            low, high = sides
    return delta


def solution(mesh):
    line = P("norm", None, "surf")
    block = P("norm", None, None, "surf")
    return jax.shard_map(
        shards,
        mesh=mesh,
        in_specs=(line, line, block, block, line, block, block, block),
        out_specs=line,
        check_vma=False,
    )
```

```python
import functools

import jax
import jax.numpy as jnp
from jax import lax
from jax.experimental import pallas as pl
from jax.experimental.pallas import tpu as pltpu
from jax.sharding import PartitionSpec as P

SWEEPS = 2
N = 48
CELLS = 4
LANES = 128
MAT = N * N
GROUPS = 32
COLS = LANES // GROUPS
ROWS = 72
FIRST = ROWS + 8
ROOM = 60
F32 = jnp.float32
BF16 = jnp.bfloat16


def params(mebibytes, microseconds):
    cost = pl.CostEstimate(flops=int(microseconds * 1e9), bytes_accessed=0, transcendentals=0)
    return dict(
        compiler_params=pltpu.CompilerParams(vmem_limit_bytes=mebibytes * 1024 * 1024), cost_estimate=cost
    )


def whole():
    return pl.BlockSpec(memory_space=pltpu.VMEM)


def matmul_cells(left, right, out, add=None):
    def block(step, carry):
        base = pl.multiple_of(step * 4 * N, 8)
        sums = [None] * 4
        for b in range(N):
            vector = right[pl.ds(b * N, N), :]
            for k in range(4):
                term = left[pl.ds(base + k * N + b, 1), :] * vector
                sums[k] = term if sums[k] is None else sums[k] + term
        for k in range(4):
            where = pl.ds(pl.multiple_of(base + k * N, 8), N)
            value = sums[k]
            if add is not None:
                value = value + add[where, :]
            out[where, :] = value
        return carry

    lax.fori_loop(0, N // 4, block, 0)


def pack_matrix(mat, out, first):
    def column(c, lo, count):
        return mat[pl.ds(c + lo * N, count, stride=N), :]

    def main(r, carry):
        tile = jnp.concatenate(
            [column(r, 0, 48), column(32 + r, 0, 16), column(16 + r, 0, 48), column(32 + r, 16, 16)], axis=0
        ).T
        for i in range(COLS):
            for g in range(0, GROUPS, 8):
                out[pl.ds(g, 8), first + i * 16 + r, :] = tile[GROUPS * i + g : GROUPS * i + g + 8]
        return carry

    lax.fori_loop(0, 16, main, 0, unroll=4)

    def rest(r, carry):
        tile = jnp.concatenate(
            [column(32 + r, 32, 16), column(40 + r, 32, 16), jnp.zeros((96, LANES), F32)], axis=0
        ).T
        line = jnp.concatenate([tile[GROUPS * i : GROUPS * (i + 1), 0:32] for i in range(COLS)], axis=1)
        for g in range(0, GROUPS, 8):
            out[pl.ds(g, 8), first + 64 + r, :] = line[g : g + 8]
        return carry

    lax.fori_loop(0, 8, rest, 0, unroll=4)


def in_hbm():
    return pl.BlockSpec(memory_space=pltpu.HBM)


def widen(narrow, wide, copies, cells):
    for k in cells:
        copies[k].wait()

        def row(r, carry):
            wide[k, pl.ds(pl.multiple_of(r * N, 16), N), :] = narrow[k, r].astype(F32)
            return carry

        lax.fori_loop(0, N, row, 0, unroll=4)


def fetch(source, target, sems, order):
    copies = {k: pltpu.make_async_copy(source.at[k], target.at[k], sems.at[k]) for k in order}
    for k in order:
        copies[k].start()
    return copies


def write_out(packed, out, rows, sem):
    copy = pltpu.make_async_copy(packed, out.at[:, pl.ds(0, rows), :] if rows < out.shape[1] else out, sem)
    copy.start()
    copy.wait()


def forward_kernel(
    rhs, delta, below, above, minus, plus, dissipation, inverse, lower, upper, after,
    out, source, chain,
    narrow, low, work, packed, sems, chain_sems, out_sem, blocks, block_sems, hold, vectors,
):
    copies = fetch(lower, narrow, sems, (0, 1, 2, 3))
    others = [
        pltpu.make_async_copy(array, blocks.at[which], block_sems.at[which])
        for which, array in enumerate((minus, plus, inverse, upper))
    ]
    for copy in others:
        copy.start()
    kept = []

    def keep(k, ref):
        kept.append(pltpu.make_async_copy(ref, chain.at[k], chain_sems.at[k]))
        kept[-1].start()

    widen(narrow, low, copies, (0, 1))
    keep(0, low.at[0])
    for k in range(1, CELLS):
        before = low.at[0] if k == 1 else work.at[k - 2]
        if k > 1:
            widen(narrow, low, copies, (k,))
        matmul_cells(low.at[k], before, work.at[k - 1])
        keep(k, work.at[k - 1])
    pack_matrix(work.at[CELLS - 2], packed, 0)
    copy = pltpu.make_async_copy(packed, out.at[:, pl.ds(0, ROWS), :], out_sem)
    copy.start()
    for other in others:
        other.wait()
    source_kernel(
        rhs, delta, below, above, blocks.at[0], blocks.at[1], dissipation, blocks.at[2], narrow, blocks.at[3],
        source, vectors, hold,
    )
    copy.wait()
    copy = pltpu.make_async_copy(vectors, out.at[:, pl.ds(ROWS, 8), :], out_sem)
    copy.start()
    copy.wait()
    for copy in kept:
        copy.wait()


def product_scratch(works):
    return [
        pltpu.VMEM((CELLS, N, N, LANES), BF16),
        pltpu.VMEM((CELLS, MAT, LANES), F32),
        pltpu.VMEM((works, MAT, LANES), F32),
        pltpu.VMEM((GROUPS, ROWS, LANES), F32),
        pltpu.SemaphoreType.DMA((CELLS,)),
        pltpu.SemaphoreType.DMA((CELLS,)),
        pltpu.SemaphoreType.DMA,
    ]


def forward_products(*arrays):
    lines = (CELLS, N, LANES)
    return pl.pallas_call(
        forward_kernel,
        out_shape=(
            jax.ShapeDtypeStruct((GROUPS, FIRST, LANES), F32),
            jax.ShapeDtypeStruct(lines, F32),
            jax.ShapeDtypeStruct((CELLS, MAT, LANES), F32),
        ),
        in_specs=[whole()] * 4 + [in_hbm()] * 2 + [whole()] + [in_hbm()] * 4,
        out_specs=(in_hbm(), whole(), in_hbm()),
        scratch_shapes=product_scratch(3)
        + [
            pltpu.VMEM((4, CELLS, N, N, LANES), BF16),
            pltpu.SemaphoreType.DMA((4,)),
            pltpu.VMEM(lines, F32),
            pltpu.VMEM((GROUPS, 8, LANES), F32),
        ],
        name="forward_products",
        **params(ROOM - 8, 17),
    )(*arrays)


def backward_kernel(upper, after, out, narrow, upp, work, packed, sems, more_sems, out_sem):
    copies = fetch(upper, narrow, sems, (3, 2, 1, 0))
    widen(narrow, upp, copies, (3, 2))
    matmul_cells(upp.at[2], upp.at[3], work.at[0])
    widen(narrow, upp, copies, (1,))
    matmul_cells(upp.at[1], work.at[0], work.at[1])
    widen(narrow, upp, copies, (0,))
    matmul_cells(upp.at[0], work.at[1], work.at[0])
    pack_matrix(work.at[0], packed, 0)
    write_out(packed, out, ROWS, out_sem)


def across_kernel(upper, after, chain, out, narrow, upp, work, packed, sems, chain_sems, out_sem, have):
    copies = fetch(upper, narrow, sems, (2,))
    chains = fetch(chain, have, chain_sems, (3, 2, 1, 0))
    copies.update(fetch(upper, narrow, sems, (1, 0)))
    widen(narrow, upp, copies, (2,))
    chains[3].wait()
    chains[2].wait()
    matmul_cells(upp.at[2], have.at[3], work.at[0], have.at[2])
    widen(narrow, upp, copies, (1,))
    chains[1].wait()
    matmul_cells(upp.at[1], work.at[0], work.at[1], have.at[1])
    widen(narrow, upp, copies, (0,))
    chains[0].wait()
    matmul_cells(upp.at[0], work.at[1], work.at[0], have.at[0])
    pack_matrix(work.at[0], packed, 0)
    write_out(packed, out, ROWS, out_sem)


def backward_products(upper, after, chain=None):
    across = chain is not None
    return pl.pallas_call(
        across_kernel if across else backward_kernel,
        out_shape=jax.ShapeDtypeStruct((GROUPS, ROWS, LANES), F32),
        in_specs=[in_hbm()] * (3 if across else 2),
        out_specs=in_hbm(),
        scratch_shapes=product_scratch(2) + [pltpu.VMEM((CELLS, MAT, LANES), F32)] * across,
        name="across_products" if across else "backward_products",
        **params(ROOM, 15),
    )(*((upper, after, chain) if across else (upper, after)))


def fold(parts):
    row = lax.broadcasted_iota(jnp.int32, (8, LANES), 0)
    for width in (4, 2, 1):
        lower_half = (row & width) == 0
        parts = [
            jnp.where(lower_half, one, two)
            + jnp.where(lower_half, pltpu.roll(one, 8 - width, 0), pltpu.roll(two, width, 0))
            for one, two in zip(parts[:width], parts[width:])
        ]
    return parts[0]


def matvec(block, vector):
    tiles = []
    for first in range(0, N, 8):
        parts = []
        for a in range(first, first + 8):
            product = block[a].astype(F32) * vector
            parts.append(sum(product[b : b + 8] for b in range(8, N, 8)) + product[0:8])
        tiles.append(fold(parts))
    return jnp.concatenate(tiles, axis=0)


def write_edges(delta, low, high):
    gap = jnp.zeros((LANES - 2 * N, LANES), F32)
    tiles = [jnp.concatenate([delta[2 * p], delta[2 * p + 1], gap], axis=0).T for p in range(2)]
    empty = jnp.zeros((4, LANES), F32)
    low[...] = jnp.concatenate([tiles[0][0:2], tiles[1][0:2], empty], axis=0)
    high[...] = jnp.concatenate([tiles[0][LANES - 2 :], tiles[1][LANES - 2 :], empty], axis=0)


def edges(delta):
    return pl.pallas_call(
        write_edges,
        out_shape=(jax.ShapeDtypeStruct((8, LANES), F32),) * 2,
        in_specs=[whole()],
        out_specs=(whole(),) * 2,
        name="edges",
        **params(4, 1),
    )(delta)


def source_kernel(
    rhs, delta, below, above, minus, plus, dissipation, inverse, lower, upper,
    source, vectors, hold,
):
    lane = lax.broadcasted_iota(jnp.int32, (N, LANES), 1)
    place = lax.axis_index("surf")
    gap = jnp.zeros((LANES - 8, LANES), F32)
    before = jnp.concatenate([jnp.where(place == 0, 0.0, below[...]), gap], axis=0).T
    after = jnp.concatenate([jnp.where(place == lax.axis_size("surf") - 1, 0.0, above[...]), gap], axis=0).T
    forward = jnp.zeros((N, LANES), F32)
    for k in range(CELLS):
        centre = delta[k]
        first = k // 2 * 2
        left = before[k % 2 * N : k % 2 * N + N]
        right = after[k % 2 * N : k % 2 * N + N]

        def shifted(by):
            here = pltpu.roll(centre, by % LANES, 1)
            if by > 0:
                return jnp.where(lane < by, pltpu.roll(left, (by - 2 - first) % LANES, 1), here)
            return jnp.where(lane >= LANES + by, pltpu.roll(right, (by - first) % LANES, 1), here)

        left_one, right_one = shifted(1), shifted(-1)
        fourth = shifted(2) - 4.0 * left_one + 6.0 * centre - 4.0 * right_one + shifted(-2)
        residual = rhs[k] - dissipation[k] * fourth
        residual = residual - matvec(minus.at[k], left_one) - matvec(plus.at[k], right_one)
        value = matvec(inverse.at[k], residual)
        source[k] = value
        forward = value + matvec(lower.at[k], forward) if k else value
        hold[k] = forward
    backward = hold[CELLS - 1]
    for k in range(CELLS - 2, -1, -1):
        backward = hold[k] + matvec(upper.at[k], backward)
    gap = jnp.zeros((16, LANES), F32)
    for row, value in ((0, forward), (COLS, backward)):
        tile = jnp.concatenate([value, gap, value, gap], axis=0).T
        for i in range(COLS):
            for g in range(0, GROUPS, 8):
                start = GROUPS * i + g
                vectors[pl.ds(g, 8), row + i, :] = tile[start : start + 8]


def local_source(*arrays):
    lines = (CELLS, N, LANES)
    return pl.pallas_call(
        source_kernel,
        out_shape=(jax.ShapeDtypeStruct(lines, F32), jax.ShapeDtypeStruct((GROUPS, 8, LANES), F32)),
        in_specs=[whole()] * 10,
        out_specs=(whole(), whole()),
        scratch_shapes=[pltpu.VMEM(lines, F32)],
        name="local_source",
        **params(16, 3),
    )(*arrays)


def finish_kernel(incoming, source, lower, upper, delta, *rest):
    hold = rest[-1]

    def incoming_line(row):
        rows = [incoming[pl.ds(row + i, GROUPS, stride=8), :] for i in range(COLS)]
        return jnp.concatenate(rows, axis=0).T[0:N]

    value = incoming_line(0)
    for k in range(CELLS):
        value = source[k] + matvec(lower.at[k], value)
        hold[k] = value
    value = incoming_line(COLS)
    for k in range(CELLS - 1, -1, -1):
        value = hold[k] + matvec(upper.at[k], value)
        delta[k] = value
    if len(rest) > 1:
        write_edges(delta, rest[0], rest[1])


def finish(last, *arrays):
    edge = jax.ShapeDtypeStruct((8, LANES), F32)
    results = (jax.ShapeDtypeStruct((CELLS, N, LANES), F32),) + (() if last else (edge, edge))
    return pl.pallas_call(
        finish_kernel,
        out_shape=results,
        in_specs=[whole()] * 4,
        out_specs=(whole(),) * len(results),
        scratch_shapes=[pltpu.VMEM((CELLS, N, LANES), F32)],
        name="finish",
        **params(8, 1.5),
    )(*arrays)


def split(value):
    high = value.astype(BF16)
    return high, (value - high.astype(F32)).astype(BF16)


def unpack_matrix(packed, d, first, weights):
    lane = lax.broadcasted_iota(jnp.int32, (16, LANES), 1)
    extra = packed[d, pl.ds(first + 64, 8), :]
    for i in range(COLS):
        block = packed[d, pl.ds(first + 16 * i, 16), :]
        turned = pltpu.roll(block, 64, 1)
        low = jnp.where(lane < 64, block, turned)
        high = jnp.where(lane < 64, turned, block)
        tail = jnp.concatenate(
            [pltpu.roll(extra, (32 - 32 * i) % LANES, 1), pltpu.roll(extra, (16 - 32 * i) % LANES, 1)], axis=0
        )
        third = jnp.where(lane < 16, pltpu.roll(block, 80, 1), jnp.where(lane < 32, pltpu.roll(block, 32, 1), tail))
        third = jnp.where(lane < 64, third, pltpu.roll(third, 64, 1))
        both = jnp.concatenate([low, high, third], axis=0)
        first_part, second_part = split(both)
        weights[pl.ds(64 * i, N), 0:LANES] = first_part
        weights[pl.ds(64 * i, N), LANES : 2 * LANES] = second_part


def clear_gaps(*weights):
    for ref in weights:
        for i in range(COLS):
            ref[pl.ds(64 * i + N, 64 - N), :] = jnp.zeros((64 - N, 2 * LANES), BF16)


def spread(value, keep):
    wide = jnp.where(keep, jnp.concatenate([value, value], axis=1), 0.0)
    high = wide.astype(BF16).astype(F32)
    return jnp.concatenate([high, wide - high], axis=0).astype(BF16)


def kept():
    row = lax.broadcasted_iota(jnp.int32, (8, 2 * LANES), 0)
    lane = lax.broadcasted_iota(jnp.int32, (8, 2 * LANES), 1)
    return jnp.logical_and(row == lane // 64, lax.rem(lane, 64) < N)


def apply(left, weights):
    out = jnp.dot(left, weights[...], preferred_element_type=F32)
    return (out[0:8, 0:LANES] + out[8:16, 0:LANES]) + (out[0:8, LANES:] + out[8:16, LANES:])


def forward_solve_kernel(packed, vectors, out, even, odd):
    weights = (even, odd)
    keep = kept()
    base = ROWS if vectors.shape[1] > 8 else 0
    clear_gaps(even, odd)
    unpack_matrix(packed, 0, 0, even)

    def pair(e, state):
        for side in range(2):
            d = 2 * e + side
            product = apply(spread(state, keep), weights[side])
            vector = vectors[d, pl.ds(base, 8), :]
            out[d, 0:8] = state
            out[d, 8:16] = vector
            unpack_matrix(packed, jnp.minimum(d + 1, GROUPS - 1), 0, weights[1 - side])
            state = vector + product
        return state

    lax.fori_loop(0, GROUPS // 2, pair, jnp.zeros((8, LANES), F32), unroll=4)


def backward_solve_kernel(packed, packed_b, states, out, even_g, odd_g, even_b, odd_b):
    weights_g, weights_b = (even_g, odd_g), (even_b, odd_b)
    row = lax.broadcasted_iota(jnp.int32, (8, LANES), 0)
    keep = kept()
    last = GROUPS - 1

    def known(d, weights):
        vector = pltpu.roll(states[d, 8:16], COLS, 0)
        return vector + apply(spread(states[d, 0:8], keep), weights)

    clear_gaps(even_g, odd_g, even_b, odd_b)
    for e in range(2):
        unpack_matrix(packed, last - e, 0, weights_g[e])
    unpack_matrix(packed_b, last, 0, even_b)

    def pair(p, carry):
        end, ready = carry
        for side in range(2):
            e = 2 * p + side
            d = last - e
            product = apply(spread(end, keep), weights_b[side])
            out[d] = jnp.where(row < COLS, states[d, 0:8], pltpu.roll(end, COLS, 0))
            after = jnp.maximum(d - 1, 0)
            end = ready + product
            ready = known(after, weights_g[1 - side])
            unpack_matrix(packed_b, after, 0, weights_b[1 - side])
            unpack_matrix(packed, jnp.maximum(d - 2, 0), 0, weights_g[side])
        return end, ready

    lax.fori_loop(0, GROUPS // 2, pair, (jnp.zeros((8, LANES), F32), known(last, even_g)), unroll=4)


def solve_kernel(packed, vectors, across, packed_b, out, *rest):
    *weights, states, held, sem = rest
    copy = pltpu.make_async_copy(across, held, sem)
    copy.start()
    forward_solve_kernel(packed, vectors, states, *weights[:2])
    copy.wait()
    backward_solve_kernel(held, packed_b, states, out, *weights[2:])


def solve_both(*arrays):
    return pl.pallas_call(
        solve_kernel,
        out_shape=jax.ShapeDtypeStruct((GROUPS, 8, LANES), F32),
        in_specs=[whole(), whole(), in_hbm(), whole()],
        out_specs=whole(),
        scratch_shapes=[pltpu.VMEM((2 * LANES, 2 * LANES), BF16)] * 6
        + [
            pltpu.VMEM((GROUPS, 16, LANES), F32),
            pltpu.VMEM((GROUPS, ROWS, LANES), F32),
            pltpu.SemaphoreType.DMA,
        ],
        name="solve_both",
        **params(12, 12),
    )(*arrays)


def solve(kernel, slots, rows, room, *arrays):
    return pl.pallas_call(
        kernel,
        out_shape=jax.ShapeDtypeStruct((GROUPS, rows, LANES), F32),
        in_specs=[whole()] * len(arrays),
        out_specs=whole(),
        scratch_shapes=[pltpu.VMEM((2 * LANES, 2 * LANES), BF16)] * slots,
        name=kernel.__name__,
        **params(room, 7),
    )(*arrays)


def exchange(value):
    return lax.all_to_all(value, "norm", 0, 0, tiled=True)


def shards(
    rhs, previous, minus_jac, plus_jac, dissipation, inverse_diag, lower_coupling, upper_coupling
):
    count = lax.axis_size("surf")
    up = [(i, (i + 1) % count) for i in range(count)]
    down = [((i + 1) % count, i) for i in range(count)]
    delta = previous
    low, high = edges(delta)
    backward_maps = backward_products(upper_coupling, low)
    for sweep_index in range(SWEEPS):
        below = lax.ppermute(high, "surf", up)
        above = lax.ppermute(low, "surf", down)
        arrays = (
            rhs, delta, below, above, minus_jac, plus_jac, dissipation, inverse_diag, lower_coupling, upper_coupling
        )
        if sweep_index == 0:
            forward_maps, source, chain = forward_products(*arrays, backward_maps)
            backward_maps = exchange(backward_maps)
            across_maps = backward_products(upper_coupling, forward_maps, chain)
            forward_maps = vectors = exchange(forward_maps)
            across_maps = exchange(across_maps)
        else:
            source, vectors = local_source(*arrays)
            vectors = exchange(vectors)
        if sweep_index == 0:
            states = solve(forward_solve_kernel, 2, 16, ROOM, forward_maps, vectors)
            incoming = solve(backward_solve_kernel, 4, 8, 8, across_maps, backward_maps, states)
        else:
            incoming = solve_both(forward_maps, vectors, across_maps, backward_maps)
        incoming = exchange(incoming)
        last = sweep_index == SWEEPS - 1
        delta, *sides = finish(
            last, incoming.reshape(GROUPS * 8, LANES), source, lower_coupling, upper_coupling
        )
        if not last:
            low, high = sides
    return delta


def solution(mesh):
    line = P("norm", None, "surf")
    block = P("norm", None, None, "surf")
    return jax.shard_map(
        shards,
        mesh=mesh,
        in_specs=(line, line, block, block, line, block, block, block),
        out_specs=line,
        check_vma=False,
    )
```
